512 devices in a mesh: seg: 32 (over z, core), sec: 16 (over y, x).
Axes of the slice: x: 4, y: 4, z: 16, core: 2. Of those that a mesh axis runs over, the one named last changes fastest.
Arguments:
- left_env: bfloat16 [32, 16, 16, 256, 256], P('seg', 'sec'), as said below
- right_env: bfloat16 [32, 16, 16, 256, 256], P('seg', 'sec'), as said below
- left_piece: bfloat16 [32, 16, 256, 256], P('seg', 'sec'), may hold values from -0.375 to 0.375
- right_piece: bfloat16 [32, 16, 256, 256], P('seg', 'sec'), may hold values from -0.375 to 0.375
- guess: bfloat16 [32, 16, 256, 256], P('seg', 'sec'), may hold values from -0.375 to 0.375
- inverse_values: float32 [32, 16, 256], P('seg', 'sec'), may hold values from 0.5 to 4
- precond: bfloat16 [32, 16, 256, 256], P('seg', 'sec'), may hold values from 0.25 to 2
- sector_rows: int32 [32, 16], P('seg', 'sec'), may hold values from 64 to 256, as said below
Outputs:
- polar_factor: float32 [32, 16, 256, 256], P('seg', 'sec')
- next_left: bfloat16 [32, 16, 256, 256], P('seg', 'sec')
- energies: float32 [32], P('seg')
The draws below stay inside these ranges and needn't reach their ends.
Inputs may be any that keep to these rules, and one draw needn't show every extreme that they name: `sector_rows`: some block has 256 live states and some has 64. `left_env`: each channel's block is symmetric. `right_env`: each channel's block is symmetric.
All inputs are finite; a program needn't handle non-finite values.
Results may differ from the reference program's by a relative error of at most 0.006.
Values may be sent and summed in bfloat16 or wider, within the bound.
A program may use at most 64 MiB of HBM per device.

```python
import math
import jax
import jax.numpy as jnp
from jax import lax

BLOCK = 256
WD = 2
ITERS = 2
NS_STEPS = 3
WT = 16
SEGS = 32
SECTORS = 16


def symmetric_env(key):
    shape = (SEGS, SECTORS, WT, BLOCK, BLOCK)
    base = jax.random.normal(key, shape, jnp.float32)
    sym = (base + jnp.swapaxes(base, -1, -2)) * 0.5 ** 0.5 * BLOCK ** (-0.5)
    return sym.astype(jnp.bfloat16)


def draw_left_env(key, part):
    return symmetric_env(jax.random.fold_in(key, 11))


def draw_right_env(key, part):
    return symmetric_env(jax.random.fold_in(key, 23))


def draw_sector_rows(key, part):
    total = SEGS * SECTORS
    rows = jax.random.randint(jax.random.fold_in(key, 31), (total,), BLOCK // 4, BLOCK + 1)
    first = jax.random.randint(jax.random.fold_in(key, 37), (), 0, total)
    second = (first + 1) % total
    rows = rows.at[first].set(BLOCK)
    rows = rows.at[second].set(BLOCK // 4)
    return rows.reshape(SEGS, SECTORS).astype(jnp.int32)


def level_of(key, extent, cuts, low, high):
    def one(position, shards_of):
        heights = jax.random.uniform(jax.random.fold_in(jax.random.fold_in(key, 6), position), (shards_of,), jnp.float32, low / len(cuts), high / len(cuts))
        return jnp.repeat(jnp.exp(heights), extent[position] // shards_of).reshape((-1,) + (1,) * (len(extent) - position - 1))

    factor_of = one(*cuts[0])
    for cut in cuts[1:]:
        factor_of = factor_of * one(*cut)
    return factor_of


def normal_values(stream_key, extent, spread, reach, cuts=(), held_as=jnp.bfloat16):
    result = jax.random.normal(stream_key, extent, jnp.float32) * spread
    if len(cuts) > 0:
        result = level_of(stream_key, extent, cuts, -0.22, 0.18) * result
    return jnp.clip(result, min=-reach, max=reach).astype(held_as)


def setup_inputs(seed: int = 0) -> dict:
    keys = jax.random.split(jax.random.key(seed), 9)
    return {
        "left_env": draw_left_env(jax.random.fold_in(keys[8], 71), 0),
        "right_env": draw_right_env(jax.random.fold_in(keys[8], 71), 0),
        "left_piece": normal_values(keys[2], (SEGS, SECTORS, BLOCK, BLOCK), BLOCK ** -0.5, 0.375, ((0, 32), (1, 16))),
        "right_piece": normal_values(keys[3], (SEGS, SECTORS, BLOCK, BLOCK), BLOCK ** -0.5, 0.375, ((0, 32), (1, 16))),
        "guess": normal_values(keys[4], (SEGS, SECTORS, BLOCK, BLOCK), BLOCK ** -0.5, 0.375, ((0, 32), (1, 16))),
        "inverse_values": jnp.clip(jnp.exp(math.log(4.0) - 2.0794415 * jax.random.uniform(keys[5], (SEGS, SECTORS, BLOCK), jnp.float32) ** level_of(keys[5], (SEGS, SECTORS, BLOCK), ((0, 32), (1, 16)), -0.2, 0.2)), 0.5, 4.0),
        "precond": jnp.clip(jnp.exp(math.log(2.0) - 2.0794415 * jax.random.uniform(keys[6], (SEGS, SECTORS, BLOCK, BLOCK), jnp.float32) ** level_of(keys[6], (SEGS, SECTORS, BLOCK, BLOCK), ((0, 32), (1, 16)), -0.2, 0.2)), 0.25, 2.0).astype(jnp.bfloat16),
        "sector_rows": draw_sector_rows(jax.random.fold_in(keys[8], 71), 0),
    }


def apply_op(vec, lenv, renv, mask):
    f32 = jnp.float32
    vb = vec.astype(jnp.bfloat16).astype(f32)
    lenv = lenv.astype(f32)
    renv = renv.astype(f32)
    inner = jnp.einsum('swij,sjk->swik', lenv[:, :WD], vb).astype(jnp.bfloat16).astype(f32)
    diag = jnp.einsum('swik,swkl->sil', inner, renv[:, :WD])
    lower = jnp.concatenate([jnp.zeros_like(vb[:1]), vb[:-1]], axis=0)
    up_inner = jnp.einsum('swij,sjk->swik', lenv[:, WD:], lower).astype(jnp.bfloat16).astype(f32)
    up = jnp.einsum('swik,swkl->sil', up_inner, renv[:, WD:])
    dn_inner = jnp.einsum('swji,sjk->swik', lenv[:, WD:], vb).astype(jnp.bfloat16).astype(f32)
    down = jnp.einsum('swik,swlk->sil', dn_inner, renv[:, WD:]).astype(jnp.bfloat16).astype(f32)
    upper = jnp.concatenate([down[1:], jnp.zeros_like(down[:1])], axis=0)
    return mask * (diag + up + upper)

def one_boundary(items):
    lenv, renv, apiece, bnext, guess, invv, precond, rows = items
    f32 = jnp.float32
    idx_r = lax.broadcasted_iota(jnp.int32, (BLOCK, BLOCK), 0)
    idx_c = lax.broadcasted_iota(jnp.int32, (BLOCK, BLOCK), 1)
    mask = ((idx_r[None] < rows[:, None, None]) & (idx_c[None] < rows[:, None, None])).astype(f32)
    scaled = (apiece.astype(f32) * invv[:, None, :]).astype(jnp.bfloat16)
    prod = jnp.einsum('sij,sjk->sik', scaled.astype(f32), bnext.astype(f32))
    start = mask * (prod + guess.astype(f32))
    x = start / jnp.sqrt(jnp.sum(start * start))
    g = apply_op(x, lenv, renv, mask)
    prec = precond.astype(f32)
    lam = jnp.float32(0.0)
    for step in range(ITERS):
        a = jnp.sum(x * g)
        p = prec * (g - a * x)
        s = jnp.sum(x * p)
        q = p - s * x
        t = q / jnp.sqrt(jnp.sum(q * q))
        h = apply_op(t, lenv, renv, mask)
        b = jnp.sum(x * h)
        c = jnp.sum(t * h)
        lam = 0.5 * (a + c) - jnp.sqrt((0.5 * (a - c)) ** 2 + b * b)
        uu = c - lam
        ww = -b
        nrm = jnp.sqrt(uu * uu + ww * ww)
        x = (uu * x + ww * t) / nrm
        g = (uu * g + ww * h) / nrm
    hi = lax.Precision.HIGHEST
    fro = lax.optimization_barrier(jnp.sum(x * x, axis=(1, 2)))
    y = x * lax.rsqrt(fro + 1e-06)[:, None, None]
    for step in range(NS_STEPS):
        gram = jnp.einsum('sij,skj->sik', y, y, precision=hi)
        y = 1.5 * y - 0.5 * jnp.einsum('sik,skj->sij', gram, y, precision=hi)
    weight = jnp.einsum('sji,sjk->sik', y, x, precision=hi).astype(jnp.bfloat16)
    return (y, weight, lam)

def reference(left_env, right_env, left_piece, right_piece, guess, inverse_values, precond, sector_rows):
    bnext = jnp.concatenate([right_piece[1:], jnp.zeros_like(right_piece[:1])], axis=0)
    polar, weight, energies = lax.map(one_boundary, (left_env, right_env, left_piece, bnext, guess, inverse_values, precond, sector_rows))
    next_left = jnp.concatenate([jnp.zeros_like(weight[:1]), weight[:-1]], axis=0)
    return (polar, next_left, energies)
```

```python
import functools

import jax
import jax.numpy as jnp
from jax import lax
from jax.experimental import pallas as pl
from jax.experimental.pallas import tpu as pltpu
from jax.sharding import PartitionSpec as P

WD = 2
ITERS = 2
NS_STEPS = 3
F32 = jnp.float32
BF16 = jnp.bfloat16
SHRINK = 2.0 ** -18
MESH = pl.DeviceIdType.MESH


def nn(a, b):
    return jnp.dot(a, b, preferred_element_type=F32)


def nt(a, b):
    return lax.dot_general(a, b, (((1,), (1,)), ((), ())), preferred_element_type=F32)


def tn(a, b):
    return lax.dot_general(a, b, (((0,), (0,)), ((), ())), preferred_element_type=F32)


def split(a):
    high = a.astype(BF16)
    return high, (a - high.astype(F32)).astype(BF16)


def three(dot, a, b):
    return dot(a[0], b[0]) + (dot(a[0], b[1]) + dot(a[1], b[0]))


def column_sum(value):
    size = value.shape[1]
    row = jnp.sum(value, axis=0, keepdims=True)
    total = row[:, :128]
    for at in range(128, size, 128):
        total = total + row[:, at:at + 128]
    return total


def kernel(
    segs, secs, lenv_hbm, renv_hbm, lpiece, rpiece_hbm, guess, inv, prec, rows,
    polar_out, handed_out, lam_out,
    lenv, renv, inner, bnext, vsend, vrecv, dsend, drecv, part, gathered, wsend,
    r_ref, g_ref, x_ref, t_ref, d_ref, zero_ref,
    load_sem, seg_send, seg_recv, v_send, v_recv, d_send, d_recv, ar_send, ar_recv, out_sem,
):
    seg = lax.axis_index("seg")
    sec = lax.axis_index("sec")
    channels, size = lenv.shape[0], lenv.shape[1]
    half = size // 2

    loads = [
        pltpu.make_async_copy(lenv_hbm.at[0, 0], lenv, load_sem.at[0]),
        pltpu.make_async_copy(renv_hbm.at[0, 0], renv, load_sem.at[1]),
    ]
    for load in loads:
        load.start()

    above = lax.rem(sec + 1, secs)
    below = lax.rem(sec + secs - 1, secs)
    ahead = lax.rem(seg + 1, segs)
    behind = lax.rem(seg + segs - 1, segs)
    barrier = pltpu.get_barrier_semaphore()
    for step in range(1, secs):
        pl.semaphore_signal(
            barrier, inc=1, device_id={"sec": lax.rem(sec + step, secs)}, device_id_type=MESH
        )
    for other in (ahead, behind):
        pl.semaphore_signal(barrier, inc=1, device_id={"seg": other}, device_id_type=MESH)
    pl.semaphore_wait(barrier, secs + 1)

    fetch = pltpu.make_async_remote_copy(
        src_ref=rpiece_hbm.at[0, 0], dst_ref=bnext, send_sem=seg_send.at[0],
        recv_sem=seg_recv.at[0], device_id={"seg": behind}, device_id_type=MESH,
    )
    fetch.start()

    count = rows[0, 0]
    idx_r = lax.broadcasted_iota(jnp.int32, (size, size), 0)
    idx_c = lax.broadcasted_iota(jnp.int32, (size, size), 1)
    alive = (idx_r < count) & (idx_c < count)
    has_below = sec > 0
    has_above = sec < secs - 1

    def up_copy(k, src, dst):
        return pltpu.make_async_remote_copy(
            src_ref=src, dst_ref=dst, send_sem=v_send.at[k], recv_sem=v_recv.at[k],
            device_id={"sec": above}, device_id_type=MESH,
        )

    def down_copy(k, src, dst):
        return pltpu.make_async_remote_copy(
            src_ref=src, dst_ref=dst, send_sem=d_send.at[k], recv_sem=d_recv.at[k],
            device_id={"sec": below}, device_id_type=MESH,
        )

    def inner_of(value, first, last):
        width = value.shape[1]
        for w in range(first, last):
            inner[:, w * size:w * size + width] = nn(lenv[w], value).astype(BF16)

    def outer_of(first, last):
        total = None
        for w in range(first, last):
            term = nn(inner[:, w * size:(w + 1) * size], renv[w])
            total = term if total is None else total + term
        return total

    def apply_op(k):
        vec = vsend[k]
        inner_of(vec, 0, channels)
        dsend[k] = outer_of(WD, channels).astype(BF16)
        down = down_copy(k, dsend.at[k], drecv.at[k])
        down.start()
        diag = outer_of(0, WD)
        return diag, down

    def finish_op(k, up, down, diag):
        up.wait_recv()
        inner_of(vrecv[k], WD, channels)
        raised = outer_of(WD, channels)
        down.wait_recv()
        lowered = drecv[k].astype(F32)
        return diag + jnp.where(has_below, raised, 0.0) + jnp.where(has_above, lowered, 0.0)

    def put(k, row, value):
        part[k, row:row + 1, :] = column_sum(value)

    def exchange(k):
        gathered[k, sec] = part[k]
        copies = []
        for step in range(1, secs):
            copy = pltpu.make_async_remote_copy(
                src_ref=part.at[k], dst_ref=gathered.at[k, sec],
                send_sem=ar_send.at[k, step], recv_sem=ar_recv.at[k, step],
                device_id={"sec": lax.rem(sec + step, secs)}, device_id_type=MESH,
            )
            copy.start()
            copies.append(copy)
        return copies

    def totals(k, copies):
        for copy in copies:
            copy.wait_recv()
        return jnp.sum(jnp.sum(gathered[k], axis=0), axis=1, keepdims=True)

    part[...] = jnp.zeros_like(part)
    d = prec[0, 0].astype(F32)
    d_ref[...] = d
    scaled = (lpiece[0, 0].astype(F32) * inv[0]).astype(BF16)
    fetch.wait_recv()
    joined = jnp.where(seg < segs - 1, nn(scaled, bnext[...]), 0.0)
    r = jnp.where(alive, joined + guess[0, 0].astype(F32), 0.0)
    r_ref[...] = r
    vsend[0] = r.astype(BF16)
    up0 = up_copy(0, vsend.at[0], vrecv.at[0])
    up0.start()
    for load in loads:
        load.wait()
    diag, down0 = apply_op(0)
    dr = d * r
    put(0, 0, r * r)
    put(0, 1, dr * r)
    put(0, 2, dr * dr)
    big_g = jnp.where(alive, SHRINK * finish_op(0, up0, down0, diag), 0.0)
    r = r_ref[...]
    d = d_ref[...]
    dr = d * r
    dg = d * big_g
    put(0, 3, r * big_g)
    put(0, 4, dr * big_g)
    put(0, 5, dg * dg)
    put(0, 6, dg * dr)
    g_ref[...] = big_g
    ex0 = exchange(0)
    tot = totals(0, ex0)
    n0 = tot[0:1]
    grow = 1.0 / SHRINK
    scale = 1.0 / jnp.sqrt(n0)
    over = 1.0 / n0
    over_g = grow * over
    x_dx = tot[1:2] * over
    dx_dx = tot[2:3] * over
    a = tot[3:4] * over_g
    x_dg = tot[4:5] * over_g
    dg_dg = tot[5:6] * over_g * grow
    dg_dx = tot[6:7] * over_g

    def correction(a, x_dx, x_dg, dx_dx, dg_dx, dg_dg):
        s = x_dg - a * x_dx
        pp = dg_dg - 2.0 * a * dg_dx + a * a * dx_dx
        qq = jnp.maximum(pp - s * s, 1e-7 * (dg_dg + a * a * dx_dx))
        return s, 1.0 / jnp.sqrt(qq)

    s, over_q = correction(a, x_dx, x_dg, dx_dx, dg_dx, dg_dg)
    x = r_ref[...] * scale
    g = g_ref[...] * (scale * grow)
    d = d_ref[...]
    t = (d * (g - a * x) - s * x) * over_q
    vsend[1] = t.astype(BF16)
    up1 = up_copy(1, vsend.at[1], vrecv.at[1])
    up1.start()
    x_ref[...] = x
    g_ref[...] = g
    t_ref[...] = t
    diag, down1 = apply_op(1)
    d = d_ref[...]
    x = x_ref[...]
    g = g_ref[...]
    t = t_ref[...]
    dt = d * t
    put(1, 0, t * t)
    put(1, 1, dt * t)
    put(1, 2, dt * x)
    put(1, 3, dt * g)
    put(1, 4, dt * dt)
    put(1, 5, dt * (d * x))
    put(1, 6, dt * (d * g))
    put(1, 7, t * g)
    h = jnp.where(alive, finish_op(1, up1, down1, diag), 0.0)
    d = d_ref[...]
    x = x_ref[...]
    g = g_ref[...]
    t = t_ref[...]
    dh = d * h
    put(1, 8, t * h)
    put(1, 9, x * h)
    put(1, 10, x * dh)
    put(1, 11, t * dh)
    put(1, 12, dh * dh)
    put(1, 13, dh * (d * g))
    put(1, 14, dh * (d * x))
    put(1, 15, dh * (d * t))
    r_ref[...] = h
    ex1 = exchange(1)
    tot = totals(1, ex1)

    def ritz(a, b, c):
        lam = 0.5 * (a + c) - jnp.sqrt((0.5 * (a - c)) ** 2 + b * b)
        u = c - lam
        w = -b
        over = 1.0 / jnp.sqrt(u * u + w * w)
        return lam, u * over, w * over

    tau = 1.0 / jnp.sqrt(tot[0:1])
    lam, al, be = ritz(a, tot[9:10] * tau, tot[8:9] * tau * tau)
    be = be * tau
    aa, ab, bb = al * al, al * be, be * be
    a = aa * a + ab * (tot[9:10] + tot[7:8]) + bb * tot[8:9]
    x_dx = aa * x_dx + 2.0 * ab * tot[2:3] + bb * tot[1:2]
    x_dg = aa * x_dg + ab * (tot[10:11] + tot[3:4]) + bb * tot[11:12]
    dg_dg = aa * dg_dg + 2.0 * ab * tot[13:14] + bb * tot[12:13]
    dg_dx = aa * dg_dx + ab * (tot[6:7] + tot[14:15]) + bb * tot[15:16]
    dx_dx = aa * dx_dx + 2.0 * ab * tot[5:6] + bb * tot[4:5]
    s, over_q = correction(a, x_dx, x_dg, dx_dx, dg_dx, dg_dg)
    x = al * x_ref[...] + be * t_ref[...]
    g = al * g_ref[...] + be * r_ref[...]
    t = (d_ref[...] * (g - a * x) - s * x) * over_q
    vsend[2] = t.astype(BF16)
    up2 = up_copy(2, vsend.at[2, :, :half], vrecv.at[2, :, :half])
    up2.start()
    x_ref[...] = x
    t_ref[...] = t
    put(2, 0, t * t)
    put(2, 1, t * g)
    inner_of(vsend[2], 0, channels)
    lower = None
    for w in range(WD, channels):
        term = nn(inner[:, w * size:(w + 1) * size], renv[w, :, half:])
        lower = term if lower is None else lower + term
    dsend[2, :, half:] = lower.astype(BF16)
    down2 = down_copy(2, dsend.at[2, :, half:], drecv.at[2, :, half:])
    down2.start()
    diag = outer_of(0, WD)
    up2.wait_recv()
    inner_of(vrecv[2, :, :half], WD, channels)
    upper = None
    for w in range(WD, channels):
        term = nn(inner[:, w * size:w * size + half], renv[w, :half, :])
        upper = term if upper is None else upper + term
    t = t_ref[...]
    put(2, 2, t * (diag + 2.0 * jnp.where(has_below, upper, 0.0)))
    down2.wait_recv()
    put(2, 3, jnp.concatenate([
        2.0 * t[:, half:] * jnp.where(has_above, drecv[2, :, half:].astype(F32), 0.0)
    ], axis=1))
    ex2 = exchange(2)
    tot = totals(2, ex2)
    tau = 1.0 / jnp.sqrt(tot[0:1])
    lam, al, be = ritz(a, tot[1:2] * tau, (tot[2:3] + tot[3:4]) * tau * tau)
    be = be * tau
    lam_out[0] = lam[0, 0]
    x = al * x_ref[...] + be * t_ref[...]
    x_ref[...] = x
    frob = jnp.sum(jnp.sum(x * x, axis=0, keepdims=True), axis=1, keepdims=True)
    polar = x * lax.rsqrt(frob + 1e-06)
    for step in range(NS_STEPS):
        pair = split(polar)
        gram = three(nt, pair, pair)
        polar = 1.5 * polar - 0.5 * three(nn, split(gram), pair)
    r_ref[...] = polar
    polar_copy = pltpu.make_async_copy(r_ref, polar_out.at[0, 0], out_sem.at[0])
    polar_copy.start()
    weight = three(tn, split(polar), split(x_ref[...]))
    wsend[...] = weight.astype(BF16)
    hand = pltpu.make_async_remote_copy(
        src_ref=wsend, dst_ref=handed_out.at[0, 0], send_sem=seg_send.at[1],
        recv_sem=seg_recv.at[1], device_id={"seg": ahead}, device_id_type=MESH,
    )

    @pl.when(seg < segs - 1)
    def _():
        hand.start()

    @pl.when(seg == 0)
    def _():
        zero_ref[...] = jnp.zeros_like(zero_ref)
        clear = pltpu.make_async_copy(zero_ref, handed_out.at[0, 0], out_sem.at[1])
        clear.start()
        clear.wait()

    fetch.wait_send()
    for copy in (up0, down0, up1, down1, up2, down2):
        copy.wait_send()
    for copy in ex0 + ex1 + ex2:
        copy.wait_send()
    polar_copy.wait()

    @pl.when(seg < segs - 1)
    def _():
        hand.wait_send()

    @pl.when(seg > 0)
    def _():
        hand.wait_recv()


def shards(segs, secs, left_env, right_env, left_piece, right_piece, guess, inverse_values,
           precond, sector_rows):
    channels, size = left_env.shape[2], left_env.shape[3]
    vmem = pl.BlockSpec(memory_space=pltpu.VMEM)
    smem = pl.BlockSpec(memory_space=pltpu.SMEM)
    hbm = pl.BlockSpec(memory_space=pl.ANY)
    square = (size, size)
    return pl.pallas_call(
        functools.partial(kernel, segs, secs),
        out_shape=(
            jax.ShapeDtypeStruct((1, 1) + square, F32),
            jax.ShapeDtypeStruct((1, 1) + square, BF16),
            jax.ShapeDtypeStruct((1,), F32),
        ),
        in_specs=[hbm, hbm, vmem, hbm, vmem, vmem, vmem, smem],
        out_specs=(hbm, hbm, smem),
        scratch_shapes=[
            pltpu.VMEM((channels,) + square, BF16),
            pltpu.VMEM((channels,) + square, BF16),
            pltpu.VMEM((size, channels * size), BF16),
            pltpu.VMEM(square, BF16),
            pltpu.VMEM((3,) + square, BF16),
            pltpu.VMEM((3,) + square, BF16),
            pltpu.VMEM((3,) + square, BF16),
            pltpu.VMEM((3,) + square, BF16),
            pltpu.VMEM((3, 16, 128), F32),
            pltpu.VMEM((3, secs, 16, 128), F32),
            pltpu.VMEM(square, BF16),
            pltpu.VMEM(square, F32),
            pltpu.VMEM(square, F32),
            pltpu.VMEM(square, F32),
            pltpu.VMEM(square, F32),
            pltpu.VMEM(square, F32),
            pltpu.VMEM(square, BF16),
            pltpu.SemaphoreType.DMA((2,)),
            pltpu.SemaphoreType.DMA((2,)),
            pltpu.SemaphoreType.DMA((2,)),
            pltpu.SemaphoreType.DMA((3,)),
            pltpu.SemaphoreType.DMA((3,)),
            pltpu.SemaphoreType.DMA((3,)),
            pltpu.SemaphoreType.DMA((3,)),
            pltpu.SemaphoreType.DMA((3, secs)),
            pltpu.SemaphoreType.DMA((3, secs)),
            pltpu.SemaphoreType.DMA((2,)),
        ],
        compiler_params=pltpu.CompilerParams(
            collective_id=0, has_side_effects=True, vmem_limit_bytes=60 * 1024 * 1024
        ),
        cost_estimate=pl.CostEstimate(
            flops=3 * 60 * 2 * size ** 3, bytes_accessed=6 * 1024 * 1024, transcendentals=0
        ),
    )(left_env, right_env, left_piece, right_piece, guess, inverse_values, precond, sector_rows)


def solution(mesh):
    placed = (
        P("seg", "sec", None, None, None),
        P("seg", "sec", None, None, None),
        P("seg", "sec", None, None),
        P("seg", "sec", None, None),
        P("seg", "sec", None, None),
        P("seg", "sec", None),
        P("seg", "sec", None, None),
        P("seg", "sec"),
    )
    return jax.shard_map(
        functools.partial(shards, mesh.shape["seg"], mesh.shape["sec"]),
        mesh=mesh,
        in_specs=placed,
        out_specs=(P("seg", "sec", None, None), P("seg", "sec", None, None), P("seg")),
        check_vma=False,
    )
```

```python
import functools

import jax
import jax.numpy as jnp
from jax import lax
from jax.experimental import pallas as pl
from jax.experimental.pallas import tpu as pltpu
from jax.sharding import PartitionSpec as P

WD = 2
ITERS = 2
NS_STEPS = 3
F32 = jnp.float32
BF16 = jnp.bfloat16
SHRINK = 2.0 ** -18
MESH = pl.DeviceIdType.MESH


def nn(a, b):
    return jnp.dot(a, b, preferred_element_type=F32)


def nt(a, b):
    return lax.dot_general(a, b, (((1,), (1,)), ((), ())), preferred_element_type=F32)


def tn(a, b):
    return lax.dot_general(a, b, (((0,), (0,)), ((), ())), preferred_element_type=F32)


def split(a):
    high = a.astype(BF16)
    return high, (a - high.astype(F32)).astype(BF16)


def three(dot, a, b):
    return dot(a[0], b[0]) + (dot(a[0], b[1]) + dot(a[1], b[0]))


def column_sum(value):
    size = value.shape[1]
    row = jnp.sum(value, axis=0, keepdims=True)
    total = row[:, :128]
    for at in range(128, size, 128):
        total = total + row[:, at:at + 128]
    return total


def kernel(
    segs, secs, lenv_hbm, renv_hbm, lpiece_hbm, rpiece_hbm, guess_hbm, inv_hbm, prec_hbm, rows_hbm,
    polar_out, handed_out, lam_out,
    lenv, renv, lpiece, guess, inv, prec, rows, inner_a, inner_b, inner_c, bnext, d_below,
    vsend, vrecv, dsend, drecv, part, gathered, wsend,
    r_ref, g_ref, e_ref, x_ref, t_ref, h_ref, d_ref, k0_ref, k1_ref, hdg_ref, dh_ref, dt_ref, zero_ref, lam_ref,
    load_sem, seg_send, seg_recv, v_send, v_recv, d_send, d_recv, ar_send, ar_recv, out_sem,
):
    seg = lax.axis_index("seg")
    sec = lax.axis_index("sec")
    channels, size = lenv.shape[0], lenv.shape[1]
    half = size // 2

    moves = (
        (rows_hbm, rows), (prec_hbm.at[0, 0], prec), (lpiece_hbm.at[0, 0], lpiece),
        (inv_hbm.at[0], inv), (guess_hbm.at[0, 0], guess), (lenv_hbm.at[0, 0], lenv),
        (renv_hbm.at[0, 0], renv),
    )
    loads = [
        pltpu.make_async_copy(src, dst, load_sem.at[at]) for at, (src, dst) in enumerate(moves)
    ]
    for load in loads:
        load.start()

    above = lax.rem(sec + 1, secs)
    below = lax.rem(sec + secs - 1, secs)
    ahead = lax.rem(seg + 1, segs)
    behind = lax.rem(seg + segs - 1, segs)
    barrier = pltpu.get_barrier_semaphore()
    for step in range(1, secs):
        pl.semaphore_signal(
            barrier, inc=1, device_id={"sec": lax.rem(sec + step, secs)}, device_id_type=MESH
        )
    for other in (ahead, behind):
        pl.semaphore_signal(barrier, inc=1, device_id={"seg": other}, device_id_type=MESH)
    part[...] = jnp.zeros_like(part)
    for load in loads[:5]:
        load.wait()
    d_ref[...] = prec[...].astype(F32)
    scaled = (lpiece[...].astype(F32) * inv[...]).astype(BF16)
    pl.semaphore_wait(barrier, secs + 1)

    fetch = pltpu.make_async_remote_copy(
        src_ref=rpiece_hbm.at[0, 0], dst_ref=bnext, send_sem=seg_send.at[0],
        recv_sem=seg_recv.at[0], device_id={"seg": behind}, device_id_type=MESH,
    )
    fetch.start()

    count = rows[0, 0]
    idx_r = lax.broadcasted_iota(jnp.int32, (size, size), 0)
    idx_c = lax.broadcasted_iota(jnp.int32, (size, size), 1)
    alive = (idx_r < count) & (idx_c < count)
    has_below = sec > 0
    has_above = sec < secs - 1
    top, bottom = slice(0, half), slice(half, size)
    sent = []

    def send(src, dst, target, send_sem, recv_sem):
        copy = pltpu.make_async_remote_copy(
            src_ref=src, dst_ref=dst, send_sem=send_sem, recv_sem=recv_sem,
            device_id=target, device_id_type=MESH,
        )
        copy.start()
        sent.append(copy)
        return copy

    def send_up(k, part_of, value):
        vsend[k, part_of] = value.astype(BF16)
        at = 2 * k + (part_of.start > 0)
        return send(
            vsend.at[k, part_of], vrecv.at[k, part_of], {"sec": above}, v_send.at[at], v_recv.at[at]
        )

    def send_down(k, part_of):
        at = 2 * k + (part_of.start > 0)
        return send(
            dsend.at[k, part_of], drecv.at[k, part_of], {"sec": below}, d_send.at[at], d_recv.at[at]
        )

    def span(first, last):
        return slice(first * size, last * size)

    def lower(k, value, part_of):
        for w in range(WD, channels):
            inner_a[part_of, span(w, w + 1)] = nn(lenv[w, part_of, :], value).astype(BF16)
        flat = renv[WD:].reshape((channels - WD) * size, size)
        dsend[k, part_of] = nn(inner_a[part_of, span(WD, channels)], flat).astype(BF16)

    def diagonal(value):
        for w in range(WD):
            inner_c[:, span(w, w + 1)] = nn(lenv[w], value).astype(BF16)
        return nn(inner_c[...], renv[:WD].reshape(WD * size, size))

    def upper(value):
        for w in range(WD, channels):
            inner_b[:, span(w, w + 1)] = nn(lenv[w], value).astype(BF16)
        return nn(inner_b[:, span(WD, channels)], renv[WD:].reshape((channels - WD) * size, size))

    def upper_part(value, part_of):
        total = None
        for w in range(WD, channels):
            moved = nn(value, renv[w]).astype(BF16)
            term = nn(lenv[w, :, part_of], moved)
            total = term if total is None else total + term
        return total

    def put(k, row, value):
        part[k, row:row + 1, :] = column_sum(value)

    def exchange(k, rows_of):
        gathered[k, sec] = part[k]
        return [
            send(
                part.at[k, :rows_of], gathered.at[k, sec, :rows_of],
                {"sec": lax.rem(sec + step, secs)}, ar_send.at[k, step], ar_recv.at[k, step],
            )
            for step in range(1, secs)
        ]

    def totals(k, copies, rows_of):
        for copy in copies:
            copy.wait_recv()
        return jnp.sum(jnp.sum(gathered[k, :, :rows_of], axis=0), axis=1, keepdims=True)

    def together(diag, raised, k):
        lowered = drecv[k].astype(F32)
        return jnp.where(
            alive,
            diag + jnp.where(has_below, raised, 0.0) + jnp.where(has_above, lowered, 0.0),
            0.0,
        )

    def raised_from(k, copies):
        copies[0].wait_recv()
        total = upper_part(vrecv[k, top], top)
        copies[1].wait_recv()
        return total + upper_part(vrecv[k, bottom], bottom)

    d_copy = send(prec, d_below, {"sec": above}, v_send.at[10], v_recv.at[10])
    fetch.wait_recv()
    up_r = []
    for part_of in (top, bottom):
        joined = jnp.where(seg < segs - 1, nn(scaled[part_of], bnext[...]), 0.0)
        value = jnp.where(alive[part_of], joined + guess[part_of].astype(F32), 0.0)
        r_ref[part_of] = value
        up_r.append(send_up(0, part_of, value))
    for load in loads[5:]:
        load.wait()
    lower(0, vsend[0], top)
    down_r = [send_down(0, top)]
    lower(0, vsend[0], bottom)
    down_r.append(send_down(0, bottom))
    h_ref[...] = diagonal(vsend[0])
    r = r_ref[...]
    e = d_ref[...] * r
    e_ref[...] = e
    vsend[1] = e.astype(BF16)
    put(0, 0, r * r)
    put(0, 1, e * r)
    put(0, 2, e * e)
    lower(1, vsend[1], top)
    lower(1, vsend[1], bottom)
    k0_ref[...] = diagonal(vsend[1])
    raised = raised_from(0, up_r)
    down_e = [send_down(1, top), send_down(1, bottom)]
    for copy in down_r:
        copy.wait_recv()
    big_g = SHRINK * together(h_ref[...], raised, 0)
    g_ref[...] = big_g
    dg = d_ref[...] * big_g
    dh_ref[...] = dg
    up_g = [send_up(2, top, dg[top]), send_up(2, bottom, dg[bottom])]
    put(0, 3, r_ref[...] * big_g)
    put(0, 4, e_ref[...] * big_g)
    put(0, 5, dg * dg)
    put(0, 6, dg * e_ref[...])
    ex0 = exchange(0, 8)
    lower(2, vsend[2], top)
    down_g = [send_down(2, top)]
    lower(2, vsend[2], bottom)
    down_g.append(send_down(2, bottom))
    k1_ref[...] = diagonal(vsend[2])
    d_copy.wait_recv()
    raised = upper((d_below[...].astype(F32) * vrecv[0].astype(F32)).astype(BF16))
    for copy in down_e:
        copy.wait_recv()
    k0_ref[...] = together(k0_ref[...], raised, 1)

    tot = totals(0, ex0, 8)
    n0 = tot[0:1]
    grow = 1.0 / SHRINK
    scale = 1.0 / jnp.sqrt(n0)
    scale_g = scale * grow
    over = 1.0 / n0
    over_g = grow * over
    x_dx = tot[1:2] * over
    dx_dx = tot[2:3] * over
    a = tot[3:4] * over_g
    x_dg = tot[4:5] * over_g
    dg_dg = tot[5:6] * over_g * grow
    dg_dx = tot[6:7] * over_g

    def correction(a, x_dx, x_dg, dx_dx, dg_dx, dg_dg):
        s = x_dg - a * x_dx
        pp = dg_dg - 2.0 * a * dg_dx + a * a * dx_dx
        qq = jnp.maximum(pp - s * s, 1e-7 * (dg_dg + a * a * dx_dx))
        return s, 1.0 / jnp.sqrt(qq)

    s, over_q = correction(a, x_dx, x_dg, dx_dx, dg_dx, dg_dg)
    s_old, q_old, a_old = s, over_q, a
    x = r_ref[...] * scale
    g = g_ref[...] * scale_g
    d = d_ref[...]
    t = (d * (g - a * x) - s * x) * over_q
    x_ref[...] = x
    g_ref[...] = g
    t_ref[...] = t
    dt = d * t
    dt_ref[...] = dt
    vsend[3] = dt.astype(BF16)
    put(1, 0, t * t)
    put(1, 1, dt * t)
    put(1, 2, dt * x)
    put(1, 3, dt * g)
    put(1, 4, dt * dt)
    put(1, 5, dt * (d * x))
    put(1, 6, dt * (d * g))
    put(1, 7, t * g)
    raised = raised_from(2, up_g)
    for copy in down_g:
        copy.wait_recv()
    hdg = together(k1_ref[...], raised, 2) * scale_g
    hdx = k0_ref[...] * scale
    hdg_ref[...] = hdg
    k0_ref[...] = hdx
    g = g_ref[...]
    h = (hdg - a * hdx - s * g) * over_q
    dh = d_ref[...] * h
    vsend[4] = dh.astype(BF16)
    up_h = send_up(4, top, dh[top])
    h_ref[...] = h
    dh_ref[...] = dh
    d = d_ref[...]
    x = x_ref[...]
    t = t_ref[...]
    put(1, 8, t * h)
    put(1, 9, x * h)
    put(1, 10, x * dh)
    put(1, 11, t * dh)
    put(1, 12, dh * dh)
    put(1, 13, dh * (d * g))
    put(1, 14, dh * (d * x))
    put(1, 15, dh * (d * t))
    ex1 = exchange(1, 16)
    lower(4, vsend[4], bottom)
    down_h = send_down(4, bottom)
    lower(3, vsend[3], bottom)
    down_t = send_down(3, bottom)
    k1_ref[...] = diagonal(vsend[4])
    r_ref[...] = diagonal(vsend[3])
    below_d = d_below[top].astype(F32)
    below_x = vrecv[0, top].astype(F32) * scale
    below_g = vrecv[2, top].astype(F32) * scale_g
    below_dt = below_d * ((below_g - (a_old * below_d + s_old) * below_x) * q_old)

    tot = totals(1, ex1, 16)

    def ritz(a, b, c):
        lam = 0.5 * (a + c) - jnp.sqrt((0.5 * (a - c)) ** 2 + b * b)
        u = c - lam
        w = -b
        over = 1.0 / jnp.sqrt(u * u + w * w)
        return lam, u * over, w * over

    tau = 1.0 / jnp.sqrt(tot[0:1])
    lam, al, be = ritz(a, tot[9:10] * tau, tot[8:9] * tau * tau)
    be = be * tau
    aa, ab, bb = al * al, al * be, be * be
    a_old = a
    a = aa * a + ab * (tot[9:10] + tot[7:8]) + bb * tot[8:9]
    x_dx = aa * x_dx + 2.0 * ab * tot[2:3] + bb * tot[1:2]
    x_dg = aa * x_dg + ab * (tot[10:11] + tot[3:4]) + bb * tot[11:12]
    dg_dg = aa * dg_dg + 2.0 * ab * tot[13:14] + bb * tot[12:13]
    dg_dx = aa * dg_dx + ab * (tot[6:7] + tot[14:15]) + bb * tot[15:16]
    dx_dx = aa * dx_dx + 2.0 * ab * tot[5:6] + bb * tot[4:5]
    s, over_q = correction(a, x_dx, x_dg, dx_dx, dg_dx, dg_dg)
    up_h.wait_recv()
    fresh_below = (vrecv[4, top].astype(F32) - a * below_dt).astype(BF16)
    raised = jnp.where(has_below, upper_part(fresh_below, top), 0.0)
    x = al * x_ref[...] + be * t_ref[...]
    g = al * g_ref[...] + be * h_ref[...]
    fresh = be * (dh_ref[...] - a * dt_ref[...])
    known = al * (d_ref[...] * (g_ref[...] - a * x_ref[...])) - s * x
    h_known = al * (hdg_ref[...] - a * k0_ref[...]) - s * g
    t = (known + fresh) * over_q
    put(2, 0, t * t)
    put(2, 1, t * g)
    x_ref[...] = x
    t_ref[...] = t
    diag = be * (k1_ref[...] - a * r_ref[...] + 2.0 * raised)
    put(2, 2, (known + 2.0 * fresh) * h_known + fresh * diag)
    down_t.wait_recv()
    down_h.wait_recv()
    lowered = drecv[4, bottom].astype(F32) - a * drecv[3, bottom].astype(F32)
    put(2, 3, fresh[bottom] * ((2.0 * be) * jnp.where(has_above, lowered, 0.0)))
    ex2 = exchange(2, 8)
    pair_x = split(x_ref[...])
    pair_t = split(t_ref[...])
    k0_ref[...] = three(nt, pair_x, pair_x)
    k1_ref[...] = three(nt, pair_x, pair_t) + three(nt, pair_t, pair_x)
    e_ref[...] = three(nt, pair_t, pair_t)
    g_ref[...] = x_ref[...].T
    h_ref[...] = t_ref[...].T
    def block_sum(value):
        return jnp.sum(jnp.sum(value, axis=0, keepdims=True), axis=1, keepdims=True)

    frob_x = block_sum(x_ref[...] * x_ref[...])
    frob_t = block_sum(t_ref[...] * t_ref[...])
    frob_xt = block_sum(x_ref[...] * t_ref[...])
    tot = totals(2, ex2, 8)
    tau = 1.0 / jnp.sqrt(tot[0:1])
    lam, al, be = ritz(a, tot[1:2] * tau, (tot[2:3] + tot[3:4]) * (over_q * tau) ** 2)
    be = be * tau
    lam_ref[0] = lam[0, 0]
    lam_copy = pltpu.make_async_copy(lam_ref, lam_out, out_sem.at[2])
    lam_copy.start()
    aa, ab, bb = al * al, al * be, be * be
    over = lax.rsqrt(aa * frob_x + 2.0 * ab * frob_xt + bb * frob_t + 1e-06)
    polar = (al * x_ref[...] + be * t_ref[...]) * over
    turned = split(al * g_ref[...] + be * h_ref[...])
    gram = (aa * k0_ref[...] + ab * k1_ref[...] + bb * e_ref[...]) * (over * over)
    for step in range(NS_STEPS):
        pair = split(polar)
        if step:
            gram = three(nt, pair, pair)
        polar = 1.5 * polar - 0.5 * three(nn, split(gram), pair)
    r_ref[...] = polar
    polar_copy = pltpu.make_async_copy(r_ref, polar_out.at[0, 0], out_sem.at[0])
    polar_copy.start()
    pair = split(polar)
    hands = []
    for at, part_of in enumerate((top, bottom)):
        weight = three(nn, (turned[0][part_of], turned[1][part_of]), pair)
        wsend[part_of] = weight.astype(BF16)
        hand = pltpu.make_async_remote_copy(
            src_ref=wsend.at[part_of], dst_ref=handed_out.at[0, 0, part_of],
            send_sem=seg_send.at[1 + at], recv_sem=seg_recv.at[1 + at],
            device_id={"seg": ahead}, device_id_type=MESH,
        )
        hands.append(hand)

        @pl.when(seg < segs - 1)
        def _():
            hand.start()

    @pl.when(seg == 0)
    def _():
        zero_ref[...] = jnp.zeros_like(zero_ref)
        clear = pltpu.make_async_copy(zero_ref, handed_out.at[0, 0], out_sem.at[1])
        clear.start()
        clear.wait()

    fetch.wait_send()
    for copy in sent:
        copy.wait_send()
    polar_copy.wait()
    lam_copy.wait()

    @pl.when(seg < segs - 1)
    def _():
        for hand in hands:
            hand.wait_send()

    @pl.when(seg > 0)
    def _():
        for hand in hands:
            hand.wait_recv()


def store(polar_in, handed_in, lam_in, polar_out, handed_out, lam_out):
    polar_out[...] = polar_in[...]
    handed_out[...] = handed_in[...]
    lam_out[0] = lam_in[0]


def shards(segs, secs, left_env, right_env, left_piece, right_piece, guess, inverse_values,
           precond, sector_rows):
    channels, size = left_env.shape[2], left_env.shape[3]
    hbm = pl.BlockSpec(memory_space=pl.ANY)
    square = (size, size)
    envs = pltpu.VMEM((channels,) + square, BF16)
    block = pltpu.VMEM(square, BF16)
    wide = pltpu.VMEM((size, channels * size), BF16)
    five = pltpu.VMEM((5,) + square, BF16)
    full = pltpu.VMEM(square, F32)
    sems = pltpu.SemaphoreType.DMA
    outs = (
        jax.ShapeDtypeStruct((1, 1) + square, F32),
        jax.ShapeDtypeStruct((1, 1) + square, BF16),
        jax.ShapeDtypeStruct((1,), F32),
    )
    made = pl.pallas_call(
        functools.partial(kernel, segs, secs),
        out_shape=outs,
        in_specs=[hbm] * 8,
        out_specs=(hbm,) * 3,
        scratch_shapes=[
            envs, envs, block, block, pltpu.VMEM((1, size), F32), block,
            pltpu.SMEM((1, 1), jnp.int32), wide, wide,
            pltpu.VMEM((size, WD * size), BF16), block, block,
            five, five, five, five,
            pltpu.VMEM((3, 16, 128), F32), pltpu.VMEM((3, secs, 16, 128), F32), block,
        ] + [full] * 12 + [
            block, pltpu.SMEM((1,), F32),
            sems((7,)), sems((3,)), sems((3,)), sems((11,)), sems((11,)), sems((10,)), sems((10,)),
            sems((3, secs)), sems((3, secs)), sems((3,)),
        ],
        compiler_params=pltpu.CompilerParams(
            collective_id=0, has_side_effects=True, vmem_limit_bytes=60 * 1024 * 1024
        ),
        cost_estimate=pl.CostEstimate(
            flops=3 * 60 * 2 * size ** 3, bytes_accessed=6 * 1024 * 1024, transcendentals=0
        ),
    )(left_env, right_env, left_piece, right_piece, guess, inverse_values, precond, sector_rows)
    vmem = pl.BlockSpec(memory_space=pltpu.VMEM)
    smem = pl.BlockSpec(memory_space=pltpu.SMEM)
    return pl.pallas_call(
        store, out_shape=outs, in_specs=[vmem, vmem, smem], out_specs=(vmem, vmem, smem)
    )(*made)


def solution(mesh):
    placed = (
        P("seg", "sec", None, None, None),
        P("seg", "sec", None, None, None),
        P("seg", "sec", None, None),
        P("seg", "sec", None, None),
        P("seg", "sec", None, None),
        P("seg", "sec", None),
        P("seg", "sec", None, None),
        P("seg", "sec"),
    )
    return jax.shard_map(
        functools.partial(shards, mesh.shape["seg"], mesh.shape["sec"]),
        mesh=mesh,
        in_specs=placed,
        out_specs=(P("seg", "sec", None, None), P("seg", "sec", None, None), P("seg")),
        check_vma=False,
    )
```

```python
import functools

import jax
import jax.numpy as jnp
from jax import lax
from jax.experimental import pallas as pl
from jax.experimental.pallas import tpu as pltpu
from jax.sharding import PartitionSpec as P

WD = 2
ITERS = 2
NS_STEPS = 3
F32 = jnp.float32
BF16 = jnp.bfloat16
SHRINK = 2.0 ** -18
MESH = pl.DeviceIdType.MESH


def nn(a, b):
    return jnp.dot(a, b, preferred_element_type=F32)


def nt(a, b):
    return lax.dot_general(a, b, (((1,), (1,)), ((), ())), preferred_element_type=F32)


def tn(a, b):
    return lax.dot_general(a, b, (((0,), (0,)), ((), ())), preferred_element_type=F32)


def split(a):
    high = a.astype(BF16)
    return high, (a - high.astype(F32)).astype(BF16)


def three(dot, a, b):
    return dot(a[0], b[0]) + (dot(a[0], b[1]) + dot(a[1], b[0]))


def column_sum(value):
    size = value.shape[1]
    row = jnp.sum(value, axis=0, keepdims=True)
    total = row[:, :128]
    for at in range(128, size, 128):
        total = total + row[:, at:at + 128]
    return total


def kernel(
    segs, secs, lenv_hbm, renv_hbm, lpiece_hbm, rpiece_hbm, guess_hbm, inv_hbm, prec_hbm, rows_hbm,
    polar_out, handed_out, lam_out,
    lenv, renv, lpiece, guess, inv, prec, rows, inner_a, inner_b, inner_c, bnext, d_below,
    vsend, vrecv, dsend, drecv, part, gathered, wsend,
    r_ref, g_ref, e_ref, x_ref, t_ref, h_ref, d_ref, k0_ref, k1_ref, hdg_ref, rh_ref, dh_ref, dt_ref, zero_ref, lam_ref,
    load_sem, seg_send, seg_recv, v_send, v_recv, d_send, d_recv, ar_send, ar_recv, out_sem,
):
    seg = lax.axis_index("seg")
    sec = lax.axis_index("sec")
    channels, size = lenv.shape[0], lenv.shape[1]
    half = size // 2

    moves = (
        (rows_hbm, rows), (prec_hbm.at[0, 0], prec), (lpiece_hbm.at[0, 0], lpiece),
        (inv_hbm.at[0], inv), (guess_hbm.at[0, 0], guess), (lenv_hbm.at[0, 0], lenv),
        (renv_hbm.at[0, 0], renv),
    )
    loads = [
        pltpu.make_async_copy(src, dst, load_sem.at[at]) for at, (src, dst) in enumerate(moves)
    ]
    for load in loads:
        load.start()

    above = lax.rem(sec + 1, secs)
    below = lax.rem(sec + secs - 1, secs)
    ahead = lax.rem(seg + 1, segs)
    behind = lax.rem(seg + segs - 1, segs)
    barrier = pltpu.get_barrier_semaphore()
    for step in range(1, secs):
        pl.semaphore_signal(
            barrier, inc=1, device_id={"sec": lax.rem(sec + step, secs)}, device_id_type=MESH
        )
    for other in (ahead, behind):
        pl.semaphore_signal(barrier, inc=1, device_id={"seg": other}, device_id_type=MESH)
    part[...] = jnp.zeros_like(part)
    for load in loads[:5]:
        load.wait()
    d_ref[...] = prec[...].astype(F32)
    scaled = (lpiece[...].astype(F32) * inv[...]).astype(BF16)
    pl.semaphore_wait(barrier, secs + 1)

    fetch = pltpu.make_async_remote_copy(
        src_ref=rpiece_hbm.at[0, 0], dst_ref=bnext, send_sem=seg_send.at[0],
        recv_sem=seg_recv.at[0], device_id={"seg": behind}, device_id_type=MESH,
    )
    fetch.start()

    count = rows[0, 0]
    idx_r = lax.broadcasted_iota(jnp.int32, (size, size), 0)
    idx_c = lax.broadcasted_iota(jnp.int32, (size, size), 1)
    alive = (idx_r < count) & (idx_c < count)
    has_below = sec > 0
    has_above = sec < secs - 1
    top, bottom = slice(0, half), slice(half, size)
    sent = []

    def send(src, dst, target, send_sem, recv_sem):
        copy = pltpu.make_async_remote_copy(
            src_ref=src, dst_ref=dst, send_sem=send_sem, recv_sem=recv_sem,
            device_id=target, device_id_type=MESH,
        )
        copy.start()
        sent.append(copy)
        return copy

    def send_up(k, part_of, value):
        vsend[k, part_of] = value.astype(BF16)
        at = 2 * k + (part_of.start > 0)
        return send(
            vsend.at[k, part_of], vrecv.at[k, part_of], {"sec": above}, v_send.at[at], v_recv.at[at]
        )

    def send_down(k, part_of):
        at = 2 * k + (part_of.start > 0)
        return send(
            dsend.at[k, part_of], drecv.at[k, part_of], {"sec": below}, d_send.at[at], d_recv.at[at]
        )

    def span(first, last):
        return slice(first * size, last * size)

    def lower(k, value, part_of):
        for w in range(WD, channels):
            inner_a[part_of, span(w, w + 1)] = nn(lenv[w, part_of, :], value).astype(BF16)
        flat = renv[WD:].reshape((channels - WD) * size, size)
        dsend[k, part_of] = nn(inner_a[part_of, span(WD, channels)], flat).astype(BF16)

    def diagonal(value):
        for w in range(WD):
            inner_c[:, span(w, w + 1)] = nn(lenv[w], value).astype(BF16)
        return nn(inner_c[...], renv[:WD].reshape(WD * size, size))

    def upper(value):
        for w in range(WD, channels):
            inner_b[:, span(w, w + 1)] = nn(lenv[w], value).astype(BF16)
        return nn(inner_b[:, span(WD, channels)], renv[WD:].reshape((channels - WD) * size, size))

    def upper_part(value, part_of):
        total = None
        for w in range(WD, channels):
            moved = nn(value, renv[w]).astype(BF16)
            term = nn(lenv[w, :, part_of], moved)
            total = term if total is None else total + term
        return total

    def put(k, row, value):
        part[k, row:row + 1, :] = column_sum(value)

    def exchange(k, rows_of):
        gathered[k, sec] = part[k]
        return [
            send(
                part.at[k, :rows_of], gathered.at[k, sec, :rows_of],
                {"sec": lax.rem(sec + step, secs)}, ar_send.at[k, step], ar_recv.at[k, step],
            )
            for step in range(1, secs)
        ]

    def totals(k, copies, rows_of):
        for copy in copies:
            copy.wait_recv()
        return jnp.sum(jnp.sum(gathered[k, :, :rows_of], axis=0), axis=1, keepdims=True)

    def together(diag, raised, k):
        lowered = drecv[k].astype(F32)
        return jnp.where(
            alive,
            diag + jnp.where(has_below, raised, 0.0) + jnp.where(has_above, lowered, 0.0),
            0.0,
        )

    def raised_from(k, copies):
        copies[0].wait_recv()
        total = upper_part(vrecv[k, top], top)
        copies[1].wait_recv()
        return total + upper_part(vrecv[k, bottom], bottom)

    d_copy = send(prec, d_below, {"sec": above}, v_send.at[10], v_recv.at[10])
    fetch.wait_recv()
    up_r = []
    for part_of in (top, bottom):
        joined = jnp.where(seg < segs - 1, nn(scaled[part_of], bnext[...]), 0.0)
        value = jnp.where(alive[part_of], joined + guess[part_of].astype(F32), 0.0)
        r_ref[part_of] = value
        up_r.append(send_up(0, part_of, value))
    for load in loads[5:]:
        load.wait()
    lower(0, vsend[0], top)
    down_r = [send_down(0, top)]
    lower(0, vsend[0], bottom)
    down_r.append(send_down(0, bottom))
    h_ref[...] = diagonal(vsend[0])
    r = r_ref[...]
    e = d_ref[...] * r
    e_ref[...] = e
    vsend[1] = e.astype(BF16)
    put(0, 0, r * r)
    put(0, 1, e * r)
    put(0, 2, e * e)
    lower(1, vsend[1], top)
    lower(1, vsend[1], bottom)
    k0_ref[...] = diagonal(vsend[1])
    raised = raised_from(0, up_r)
    down_e = [send_down(1, top), send_down(1, bottom)]
    for copy in down_r:
        copy.wait_recv()
    big_g = SHRINK * together(h_ref[...], raised, 0)
    g_ref[...] = big_g
    dg = d_ref[...] * big_g
    dh_ref[...] = dg
    put(0, 3, r_ref[...] * big_g)
    put(0, 4, e_ref[...] * big_g)
    put(0, 5, dg * dg)
    put(0, 6, dg * e_ref[...])
    ex0 = exchange(0, 8)
    dg = dh_ref[...]
    up_g = [send_up(2, top, dg[top]), send_up(2, bottom, dg[bottom])]
    lower(2, vsend[2], top)
    down_g = [send_down(2, top)]
    lower(2, vsend[2], bottom)
    down_g.append(send_down(2, bottom))
    k1_ref[...] = diagonal(vsend[2])
    d_copy.wait_recv()
    raised = upper((d_below[...].astype(F32) * vrecv[0].astype(F32)).astype(BF16))
    for copy in down_e:
        copy.wait_recv()
    k0_ref[...] = together(k0_ref[...], raised, 1)
    up_g[0].wait_recv()
    h_ref[...] = upper_part(vrecv[2, top], top)

    tot = totals(0, ex0, 8)
    up_g[1].wait_recv()
    raised = h_ref[...] + upper_part(vrecv[2, bottom], bottom)
    n0 = tot[0:1]
    grow = 1.0 / SHRINK
    scale = 1.0 / jnp.sqrt(n0)
    scale_g = scale * grow
    over = 1.0 / n0
    over_g = grow * over
    x_dx = tot[1:2] * over
    dx_dx = tot[2:3] * over
    a = tot[3:4] * over_g
    x_dg = tot[4:5] * over_g
    dg_dg = tot[5:6] * over_g * grow
    dg_dx = tot[6:7] * over_g

    def correction(a, x_dx, x_dg, dx_dx, dg_dx, dg_dg):
        s = x_dg - a * x_dx
        pp = dg_dg - 2.0 * a * dg_dx + a * a * dx_dx
        qq = jnp.maximum(pp - s * s, 1e-7 * (dg_dg + a * a * dx_dx))
        return s, 1.0 / jnp.sqrt(qq)

    s, over_q = correction(a, x_dx, x_dg, dx_dx, dg_dx, dg_dg)
    s_old, q_old, a_old = s, over_q, a
    x = r_ref[...] * scale
    g = g_ref[...] * scale_g
    d = d_ref[...]
    t = (d * (g - a * x) - s * x) * over_q
    x_ref[...] = x
    g_ref[...] = g
    t_ref[...] = t
    dt = d * t
    dt_ref[...] = dt
    vsend[3] = dt.astype(BF16)
    put(1, 0, t * t)
    put(1, 1, dt * t)
    put(1, 2, dt * x)
    put(1, 3, dt * g)
    put(1, 4, dt * dt)
    put(1, 5, dt * (d * x))
    put(1, 6, dt * (d * g))
    put(1, 7, t * g)
    for copy in down_g:
        copy.wait_recv()
    hdg = together(k1_ref[...], raised, 2) * scale_g
    hdx = k0_ref[...] * scale
    hdg_ref[...] = hdg
    k0_ref[...] = hdx
    g = g_ref[...]
    h = (hdg - a * hdx - s * g) * over_q
    dh = d_ref[...] * h
    h_ref[...] = h
    dh_ref[...] = dh
    d = d_ref[...]
    x = x_ref[...]
    t = t_ref[...]
    put(1, 8, t * h)
    put(1, 9, x * h)
    put(1, 10, x * dh)
    put(1, 11, t * dh)
    put(1, 12, dh * dh)
    put(1, 13, dh * (d * g))
    put(1, 14, dh * (d * x))
    put(1, 15, dh * (d * t))
    ex1 = exchange(1, 16)
    dh = dh_ref[...]
    vsend[4] = dh.astype(BF16)
    up_h = send(
        vsend.at[4, top], vrecv.at[4, top], {"sec": above}, v_send.at[8], v_recv.at[8]
    )
    lower(4, vsend[4], bottom)
    down_h = send_down(4, bottom)
    lower(3, vsend[3], bottom)
    down_t = send_down(3, bottom)
    k1_ref[...] = diagonal(vsend[4])
    r_ref[...] = diagonal(vsend[3])
    below_d = d_below[top].astype(F32)
    below_x = vrecv[0, top].astype(F32) * scale
    below_g = vrecv[2, top].astype(F32) * scale_g
    below_dt = below_d * ((below_g - (a_old * below_d + s_old) * below_x) * q_old)
    e_ref[...] = upper_part(below_dt.astype(BF16), top)
    up_h.wait_recv()
    rh_ref[...] = upper_part(vrecv[4, top], top)

    tot = totals(1, ex1, 16)

    def ritz(a, b, c):
        lam = 0.5 * (a + c) - jnp.sqrt((0.5 * (a - c)) ** 2 + b * b)
        u = c - lam
        w = -b
        over = 1.0 / jnp.sqrt(u * u + w * w)
        return lam, u * over, w * over

    tau = 1.0 / jnp.sqrt(tot[0:1])
    lam, al, be = ritz(a, tot[9:10] * tau, tot[8:9] * tau * tau)
    be = be * tau
    aa, ab, bb = al * al, al * be, be * be
    a_old = a
    a = aa * a + ab * (tot[9:10] + tot[7:8]) + bb * tot[8:9]
    x_dx = aa * x_dx + 2.0 * ab * tot[2:3] + bb * tot[1:2]
    x_dg = aa * x_dg + ab * (tot[10:11] + tot[3:4]) + bb * tot[11:12]
    dg_dg = aa * dg_dg + 2.0 * ab * tot[13:14] + bb * tot[12:13]
    dg_dx = aa * dg_dx + ab * (tot[6:7] + tot[14:15]) + bb * tot[15:16]
    dx_dx = aa * dx_dx + 2.0 * ab * tot[5:6] + bb * tot[4:5]
    s, over_q = correction(a, x_dx, x_dg, dx_dx, dg_dx, dg_dg)
    raised = jnp.where(has_below, rh_ref[...] - a * e_ref[...], 0.0)
    x = al * x_ref[...] + be * t_ref[...]
    g = al * g_ref[...] + be * h_ref[...]
    fresh = be * (dh_ref[...] - a * dt_ref[...])
    known = al * (d_ref[...] * (g_ref[...] - a * x_ref[...])) - s * x
    h_known = al * (hdg_ref[...] - a * k0_ref[...]) - s * g
    t = (known + fresh) * over_q
    put(2, 0, t * t)
    put(2, 1, t * g)
    x_ref[...] = x
    t_ref[...] = t
    diag = be * (k1_ref[...] - a * r_ref[...] + 2.0 * raised)
    put(2, 2, (known + 2.0 * fresh) * h_known + fresh * diag)
    down_t.wait_recv()
    down_h.wait_recv()
    lowered = drecv[4, bottom].astype(F32) - a * drecv[3, bottom].astype(F32)
    put(2, 3, fresh[bottom] * ((2.0 * be) * jnp.where(has_above, lowered, 0.0)))
    ex2 = exchange(2, 8)
    pair_x = split(x_ref[...])
    pair_t = split(t_ref[...])
    k0_ref[...] = three(nt, pair_x, pair_x)
    k1_ref[...] = three(nt, pair_x, pair_t) + three(nt, pair_t, pair_x)
    e_ref[...] = three(nt, pair_t, pair_t)
    g_ref[...] = x_ref[...].T
    h_ref[...] = t_ref[...].T
    def block_sum(value):
        return jnp.sum(jnp.sum(value, axis=0, keepdims=True), axis=1, keepdims=True)

    frob_x = block_sum(x_ref[...] * x_ref[...])
    frob_t = block_sum(t_ref[...] * t_ref[...])
    frob_xt = block_sum(x_ref[...] * t_ref[...])
    tot = totals(2, ex2, 8)
    tau = 1.0 / jnp.sqrt(tot[0:1])
    lam, al, be = ritz(a, tot[1:2] * tau, (tot[2:3] + tot[3:4]) * (over_q * tau) ** 2)
    be = be * tau
    lam_ref[0] = lam[0, 0]
    lam_copy = pltpu.make_async_copy(lam_ref, lam_out, out_sem.at[2])
    lam_copy.start()
    aa, ab, bb = al * al, al * be, be * be
    over = lax.rsqrt(aa * frob_x + 2.0 * ab * frob_xt + bb * frob_t + 1e-06)
    polar = (al * x_ref[...] + be * t_ref[...]) * over
    turned = split(al * g_ref[...] + be * h_ref[...])
    gram = (aa * k0_ref[...] + ab * k1_ref[...] + bb * e_ref[...]) * (over * over)
    for step in range(NS_STEPS):
        near = polar.astype(BF16)
        if step:
            gram = nt(near, near)
        polar = 1.5 * polar - 0.5 * nn(gram.astype(BF16), near)
    r_ref[...] = polar
    polar_copy = pltpu.make_async_copy(r_ref, polar_out.at[0, 0], out_sem.at[0])
    polar_copy.start()
    pair = split(polar)
    hands = []
    for at, part_of in enumerate((top, bottom)):
        weight = three(nn, (turned[0][part_of], turned[1][part_of]), pair)
        wsend[part_of] = weight.astype(BF16)
        hand = pltpu.make_async_remote_copy(
            src_ref=wsend.at[part_of], dst_ref=handed_out.at[0, 0, part_of],
            send_sem=seg_send.at[1 + at], recv_sem=seg_recv.at[1 + at],
            device_id={"seg": ahead}, device_id_type=MESH,
        )
        hands.append(hand)

        @pl.when(seg < segs - 1)
        def _():
            hand.start()

    @pl.when(seg == 0)
    def _():
        zero_ref[...] = jnp.zeros_like(zero_ref)
        clear = pltpu.make_async_copy(zero_ref, handed_out.at[0, 0], out_sem.at[1])
        clear.start()
        clear.wait()

    fetch.wait_send()
    for copy in sent:
        copy.wait_send()
    polar_copy.wait()
    lam_copy.wait()

    @pl.when(seg < segs - 1)
    def _():
        for hand in hands:
            hand.wait_send()

    @pl.when(seg > 0)
    def _():
        for hand in hands:
            hand.wait_recv()


def store(polar_in, handed_in, lam_in, polar_out, handed_out, lam_out):
    polar_out[...] = polar_in[...]
    handed_out[...] = handed_in[...]
    lam_out[0] = lam_in[0]


def shards(segs, secs, left_env, right_env, left_piece, right_piece, guess, inverse_values,
           precond, sector_rows):
    channels, size = left_env.shape[2], left_env.shape[3]
    hbm = pl.BlockSpec(memory_space=pl.ANY)
    square = (size, size)
    envs = pltpu.VMEM((channels,) + square, BF16)
    block = pltpu.VMEM(square, BF16)
    wide = pltpu.VMEM((size, channels * size), BF16)
    five = pltpu.VMEM((5,) + square, BF16)
    full = pltpu.VMEM(square, F32)
    sems = pltpu.SemaphoreType.DMA
    outs = (
        jax.ShapeDtypeStruct((1, 1) + square, F32),
        jax.ShapeDtypeStruct((1, 1) + square, BF16),
        jax.ShapeDtypeStruct((1,), F32),
    )
    made = pl.pallas_call(
        functools.partial(kernel, segs, secs),
        out_shape=outs,
        in_specs=[hbm] * 8,
        out_specs=(hbm,) * 3,
        scratch_shapes=[
            envs, envs, block, block, pltpu.VMEM((1, size), F32), block,
            pltpu.SMEM((1, 1), jnp.int32), wide, wide,
            pltpu.VMEM((size, WD * size), BF16), block, block,
            five, five, five, five,
            pltpu.VMEM((3, 16, 128), F32), pltpu.VMEM((3, secs, 16, 128), F32), block,
        ] + [full] * 13 + [
            block, pltpu.SMEM((1,), F32),
            sems((7,)), sems((3,)), sems((3,)), sems((11,)), sems((11,)), sems((10,)), sems((10,)),
            sems((3, secs)), sems((3, secs)), sems((3,)),
        ],
        compiler_params=pltpu.CompilerParams(
            collective_id=0, has_side_effects=True, vmem_limit_bytes=60 * 1024 * 1024
        ),
        cost_estimate=pl.CostEstimate(
            flops=3 * 60 * 2 * size ** 3, bytes_accessed=6 * 1024 * 1024, transcendentals=0
        ),
    )(left_env, right_env, left_piece, right_piece, guess, inverse_values, precond, sector_rows)
    vmem = pl.BlockSpec(memory_space=pltpu.VMEM)
    smem = pl.BlockSpec(memory_space=pltpu.SMEM)
    return pl.pallas_call(
        store, out_shape=outs, in_specs=[vmem, vmem, smem], out_specs=(vmem, vmem, smem)
    )(*made)


def solution(mesh):
    placed = (
        P("seg", "sec", None, None, None),
        P("seg", "sec", None, None, None),
        P("seg", "sec", None, None),
        P("seg", "sec", None, None),
        P("seg", "sec", None, None),
        P("seg", "sec", None),
        P("seg", "sec", None, None),
        P("seg", "sec"),
    )
    return jax.shard_map(
        functools.partial(shards, mesh.shape["seg"], mesh.shape["sec"]),
        mesh=mesh,
        in_specs=placed,
        out_specs=(P("seg", "sec", None, None), P("seg", "sec", None, None), P("seg")),
        check_vma=False,
    )
```

```python
import functools

import jax
import jax.numpy as jnp
from jax import lax
from jax.experimental import pallas as pl
from jax.experimental.pallas import tpu as pltpu
from jax.sharding import PartitionSpec as P

WD = 2
ITERS = 2
NS_STEPS = 3
F32 = jnp.float32
BF16 = jnp.bfloat16
SHRINK = 2.0 ** -18
MESH = pl.DeviceIdType.MESH


def nn(a, b):
    return jnp.dot(a, b, preferred_element_type=F32)


def nt(a, b):
    return lax.dot_general(a, b, (((1,), (1,)), ((), ())), preferred_element_type=F32)


def tn(a, b):
    return lax.dot_general(a, b, (((0,), (0,)), ((), ())), preferred_element_type=F32)


def split(a):
    high = a.astype(BF16)
    return high, (a - high.astype(F32)).astype(BF16)


def three(dot, a, b):
    return dot(a[0], b[0]) + (dot(a[0], b[1]) + dot(a[1], b[0]))


def column_sum(value):
    size = value.shape[1]
    row = jnp.sum(value, axis=0, keepdims=True)
    total = row[:, :128]
    for at in range(128, size, 128):
        total = total + row[:, at:at + 128]
    return total


def kernel(
    segs, secs, lenv_hbm, renv_hbm, lpiece_hbm, rpiece_hbm, guess_hbm, inv_hbm, prec_hbm, rows_hbm,
    polar_out, handed_out, lam_out,
    lenv, renv, lpiece, guess, inv, prec, rows, inner_a, inner_b, inner_c, bnext, d_below,
    vsend, vrecv, dsend, drecv, part, gathered, wsend,
    r_ref, g_ref, e_ref, x_ref, t_ref, h_ref, d_ref, k0_ref, k1_ref, hdg_ref, rh_ref, dh_ref, dt_ref, zero_ref, lam_ref,
    load_sem, seg_send, seg_recv, v_send, v_recv, d_send, d_recv, ar_send, ar_recv, out_sem,
):
    seg = lax.axis_index("seg")
    sec = lax.axis_index("sec")
    channels, size = lenv.shape[0], lenv.shape[1]
    half = size // 2

    moves = (
        (rows_hbm, rows), (prec_hbm.at[0, 0], prec), (lpiece_hbm.at[0, 0], lpiece),
        (inv_hbm.at[0], inv), (guess_hbm.at[0, 0], guess), (lenv_hbm.at[0, 0], lenv),
        (renv_hbm.at[0, 0], renv),
    )
    loads = [
        pltpu.make_async_copy(src, dst, load_sem.at[at]) for at, (src, dst) in enumerate(moves)
    ]
    for load in loads:
        load.start()

    above = lax.rem(sec + 1, secs)
    below = lax.rem(sec + secs - 1, secs)
    ahead = lax.rem(seg + 1, segs)
    behind = lax.rem(seg + segs - 1, segs)
    barrier = pltpu.get_barrier_semaphore()
    for step in range(1, secs):
        pl.semaphore_signal(
            barrier, inc=1, device_id={"sec": lax.rem(sec + step, secs)}, device_id_type=MESH
        )
    for other in (ahead, behind):
        pl.semaphore_signal(barrier, inc=1, device_id={"seg": other}, device_id_type=MESH)
    part[...] = jnp.zeros_like(part)
    for load in loads[:5]:
        load.wait()
    d_ref[...] = prec[...].astype(F32)
    scaled = (lpiece[...].astype(F32) * inv[...]).astype(BF16)
    pl.semaphore_wait(barrier, secs + 1)

    fetch = pltpu.make_async_remote_copy(
        src_ref=rpiece_hbm.at[0, 0], dst_ref=bnext, send_sem=seg_send.at[0],
        recv_sem=seg_recv.at[0], device_id={"seg": behind}, device_id_type=MESH,
    )
    fetch.start()

    count = rows[0, 0]
    idx_r = lax.broadcasted_iota(jnp.int32, (size, size), 0)
    idx_c = lax.broadcasted_iota(jnp.int32, (size, size), 1)
    alive = (idx_r < count) & (idx_c < count)
    has_below = sec > 0
    has_above = sec < secs - 1
    top, bottom = slice(0, half), slice(half, size)
    sent = []

    def send(src, dst, target, send_sem, recv_sem):
        copy = pltpu.make_async_remote_copy(
            src_ref=src, dst_ref=dst, send_sem=send_sem, recv_sem=recv_sem,
            device_id=target, device_id_type=MESH,
        )
        copy.start()
        sent.append(copy)
        return copy

    def send_up(k, part_of, value):
        vsend[k, part_of] = value.astype(BF16)
        at = 2 * k + (part_of.start > 0)
        return send(
            vsend.at[k, part_of], vrecv.at[k, part_of], {"sec": above}, v_send.at[at], v_recv.at[at]
        )

    def send_down(k, part_of):
        at = 2 * k + (part_of.start > 0)
        return send(
            dsend.at[k, part_of], drecv.at[k, part_of], {"sec": below}, d_send.at[at], d_recv.at[at]
        )

    def span(first, last):
        return slice(first * size, last * size)

    def lower(k, value, part_of):
        for w in range(WD, channels):
            inner_a[part_of, span(w, w + 1)] = nn(lenv[w, part_of, :], value).astype(BF16)
        flat = renv[WD:].reshape((channels - WD) * size, size)
        dsend[k, part_of] = nn(inner_a[part_of, span(WD, channels)], flat).astype(BF16)

    def diagonal(value):
        for w in range(WD):
            inner_c[:, span(w, w + 1)] = nn(lenv[w], value).astype(BF16)
        return nn(inner_c[...], renv[:WD].reshape(WD * size, size))

    def upper(value):
        for w in range(WD, channels):
            inner_b[:, span(w, w + 1)] = nn(lenv[w], value).astype(BF16)
        return nn(inner_b[:, span(WD, channels)], renv[WD:].reshape((channels - WD) * size, size))

    def upper_part(value, part_of):
        total = None
        for w in range(WD, channels):
            moved = nn(value, renv[w]).astype(BF16)
            term = nn(lenv[w, :, part_of], moved)
            total = term if total is None else total + term
        return total

    def put(k, row, value):
        part[k, row:row + 1, :] = column_sum(value)

    def exchange(k, rows_of):
        gathered[k, sec] = part[k]
        return [
            send(
                part.at[k, :rows_of], gathered.at[k, sec, :rows_of],
                {"sec": lax.rem(sec + step, secs)}, ar_send.at[k, step], ar_recv.at[k, step],
            )
            for step in range(1, secs)
        ]

    def totals(k, copies, rows_of):
        for copy in copies:
            copy.wait_recv()
        return jnp.sum(jnp.sum(gathered[k, :, :rows_of], axis=0), axis=1, keepdims=True)

    def together(diag, raised, k):
        lowered = drecv[k].astype(F32)
        return jnp.where(
            alive,
            diag + jnp.where(has_below, raised, 0.0) + jnp.where(has_above, lowered, 0.0),
            0.0,
        )

    def raised_from(k, copies):
        copies[0].wait_recv()
        total = upper_part(vrecv[k, top], top)
        copies[1].wait_recv()
        return total + upper_part(vrecv[k, bottom], bottom)

    d_copy = send(prec, d_below, {"sec": above}, v_send.at[10], v_recv.at[10])
    fetch.wait_recv()
    up_r = []
    for part_of in (top, bottom):
        joined = jnp.where(seg < segs - 1, nn(scaled[part_of], bnext[...]), 0.0)
        value = jnp.where(alive[part_of], joined + guess[part_of].astype(F32), 0.0)
        r_ref[part_of] = value
        up_r.append(send_up(0, part_of, value))
    for load in loads[5:]:
        load.wait()
    lower(0, vsend[0], top)
    down_r = [send_down(0, top)]
    lower(0, vsend[0], bottom)
    down_r.append(send_down(0, bottom))
    h_ref[...] = diagonal(vsend[0])
    r = r_ref[...]
    e = d_ref[...] * r
    e_ref[...] = e
    vsend[1] = e.astype(BF16)
    put(0, 0, r * r)
    put(0, 1, e * r)
    put(0, 2, e * e)
    lower(1, vsend[1], top)
    lower(1, vsend[1], bottom)
    k0_ref[...] = diagonal(vsend[1])
    raised = raised_from(0, up_r)
    down_e = [send_down(1, top), send_down(1, bottom)]
    for copy in down_r:
        copy.wait_recv()
    big_g = SHRINK * together(h_ref[...], raised, 0)
    g_ref[...] = big_g
    dg = d_ref[...] * big_g
    dh_ref[...] = dg
    put(0, 3, r_ref[...] * big_g)
    put(0, 4, e_ref[...] * big_g)
    put(0, 5, dg * dg)
    put(0, 6, dg * e_ref[...])
    ex0 = exchange(0, 8)
    dg = dh_ref[...]
    up_g = [send_up(2, top, dg[top]), send_up(2, bottom, dg[bottom])]
    lower(2, vsend[2], top)
    down_g = [send_down(2, top)]
    lower(2, vsend[2], bottom)
    down_g.append(send_down(2, bottom))
    k1_ref[...] = diagonal(vsend[2])
    d_copy.wait_recv()
    raised = upper((d_below[...].astype(F32) * vrecv[0].astype(F32)).astype(BF16))
    for copy in down_e:
        copy.wait_recv()
    k0_ref[...] = together(k0_ref[...], raised, 1)
    up_g[0].wait_recv()
    h_ref[...] = upper_part(vrecv[2, top], top)

    tot = totals(0, ex0, 8)
    up_g[1].wait_recv()
    raised = h_ref[...] + upper_part(vrecv[2, bottom], bottom)
    n0 = tot[0:1]
    grow = 1.0 / SHRINK
    scale = 1.0 / jnp.sqrt(n0)
    scale_g = scale * grow
    over = 1.0 / n0
    over_g = grow * over
    x_dx = tot[1:2] * over
    dx_dx = tot[2:3] * over
    a = tot[3:4] * over_g
    x_dg = tot[4:5] * over_g
    dg_dg = tot[5:6] * over_g * grow
    dg_dx = tot[6:7] * over_g

    def correction(a, x_dx, x_dg, dx_dx, dg_dx, dg_dg):
        s = x_dg - a * x_dx
        pp = dg_dg - 2.0 * a * dg_dx + a * a * dx_dx
        qq = jnp.maximum(pp - s * s, 1e-7 * (dg_dg + a * a * dx_dx))
        return s, 1.0 / jnp.sqrt(qq)

    s, over_q = correction(a, x_dx, x_dg, dx_dx, dg_dx, dg_dg)
    s_old, q_old, a_old = s, over_q, a
    x = r_ref[...] * scale
    g = g_ref[...] * scale_g
    d = d_ref[...]
    t = (d * (g - a * x) - s * x) * over_q
    x_ref[...] = x
    g_ref[...] = g
    t_ref[...] = t
    dt = d * t
    dt_ref[...] = dt
    vsend[3] = dt.astype(BF16)
    put(1, 0, t * t)
    put(1, 1, dt * t)
    put(1, 2, dt * x)
    put(1, 3, dt * g)
    put(1, 4, dt * dt)
    put(1, 5, dt * (d * x))
    put(1, 6, dt * (d * g))
    put(1, 7, t * g)
    for copy in down_g:
        copy.wait_recv()
    hdg = together(k1_ref[...], raised, 2) * scale_g
    hdx = k0_ref[...] * scale
    hdg_ref[...] = hdg
    k0_ref[...] = hdx
    lower(3, vsend[3], bottom)
    r_ref[...] = diagonal(vsend[3])
    g = g_ref[...]
    h = (hdg - a * hdx - s * g) * over_q
    dh = d_ref[...] * h
    h_ref[...] = h
    dh_ref[...] = dh
    d = d_ref[...]
    x = x_ref[...]
    t = t_ref[...]
    put(1, 8, t * h)
    put(1, 9, x * h)
    put(1, 10, x * dh)
    put(1, 11, t * dh)
    put(1, 12, dh * dh)
    put(1, 13, dh * (d * g))
    put(1, 14, dh * (d * x))
    put(1, 15, dh * (d * t))
    ex1 = exchange(1, 16)
    dh = dh_ref[...]
    vsend[4] = dh.astype(BF16)
    up_h = send(
        vsend.at[4, top], vrecv.at[4, top], {"sec": above}, v_send.at[8], v_recv.at[8]
    )
    lower(4, vsend[4], bottom)
    down_h = send_down(4, bottom)
    down_t = send_down(3, bottom)
    k1_ref[...] = diagonal(vsend[4])
    below_d = d_below[top].astype(F32)
    below_x = vrecv[0, top].astype(F32) * scale
    below_g = vrecv[2, top].astype(F32) * scale_g
    below_dt = below_d * ((below_g - (a_old * below_d + s_old) * below_x) * q_old)
    e_ref[...] = upper_part(below_dt.astype(BF16), top)
    up_h.wait_recv()
    rh_ref[...] = upper_part(vrecv[4, top], top)

    tot = totals(1, ex1, 16)

    def ritz(a, b, c):
        lam = 0.5 * (a + c) - jnp.sqrt((0.5 * (a - c)) ** 2 + b * b)
        u = c - lam
        w = -b
        over = 1.0 / jnp.sqrt(u * u + w * w)
        return lam, u * over, w * over

    tau = 1.0 / jnp.sqrt(tot[0:1])
    lam, al, be = ritz(a, tot[9:10] * tau, tot[8:9] * tau * tau)
    be = be * tau
    aa, ab, bb = al * al, al * be, be * be
    a_old = a
    a = aa * a + ab * (tot[9:10] + tot[7:8]) + bb * tot[8:9]
    x_dx = aa * x_dx + 2.0 * ab * tot[2:3] + bb * tot[1:2]
    x_dg = aa * x_dg + ab * (tot[10:11] + tot[3:4]) + bb * tot[11:12]
    dg_dg = aa * dg_dg + 2.0 * ab * tot[13:14] + bb * tot[12:13]
    dg_dx = aa * dg_dx + ab * (tot[6:7] + tot[14:15]) + bb * tot[15:16]
    dx_dx = aa * dx_dx + 2.0 * ab * tot[5:6] + bb * tot[4:5]
    s, over_q = correction(a, x_dx, x_dg, dx_dx, dg_dx, dg_dg)
    raised = jnp.where(has_below, rh_ref[...] - a * e_ref[...], 0.0)
    x = al * x_ref[...] + be * t_ref[...]
    g = al * g_ref[...] + be * h_ref[...]
    fresh = be * (dh_ref[...] - a * dt_ref[...])
    known = al * (d_ref[...] * (g_ref[...] - a * x_ref[...])) - s * x
    h_known = al * (hdg_ref[...] - a * k0_ref[...]) - s * g
    t = (known + fresh) * over_q
    put(2, 0, t * t)
    put(2, 1, t * g)
    x_ref[...] = x
    t_ref[...] = t
    diag = be * (k1_ref[...] - a * r_ref[...] + 2.0 * raised)
    put(2, 2, (known + 2.0 * fresh) * h_known + fresh * diag)
    down_t.wait_recv()
    down_h.wait_recv()
    lowered = drecv[4, bottom].astype(F32) - a * drecv[3, bottom].astype(F32)
    put(2, 3, fresh[bottom] * ((2.0 * be) * jnp.where(has_above, lowered, 0.0)))
    ex2 = exchange(2, 8)
    pair_x = split(x_ref[...])
    pair_t = split(t_ref[...])
    k0_ref[...] = three(nt, pair_x, pair_x)
    k1_ref[...] = three(nt, pair_x, pair_t) + three(nt, pair_t, pair_x)
    e_ref[...] = three(nt, pair_t, pair_t)
    g_ref[...] = x_ref[...].T
    h_ref[...] = t_ref[...].T
    def block_sum(value):
        return jnp.sum(jnp.sum(value, axis=0, keepdims=True), axis=1, keepdims=True)

    frob_x = block_sum(x_ref[...] * x_ref[...])
    frob_t = block_sum(t_ref[...] * t_ref[...])
    frob_xt = block_sum(x_ref[...] * t_ref[...])
    tot = totals(2, ex2, 8)
    tau = 1.0 / jnp.sqrt(tot[0:1])
    lam, al, be = ritz(a, tot[1:2] * tau, (tot[2:3] + tot[3:4]) * (over_q * tau) ** 2)
    be = be * tau
    lam_ref[0] = lam[0, 0]
    lam_copy = pltpu.make_async_copy(lam_ref, lam_out, out_sem.at[2])
    lam_copy.start()
    aa, ab, bb = al * al, al * be, be * be
    over = lax.rsqrt(aa * frob_x + 2.0 * ab * frob_xt + bb * frob_t + 1e-06)
    polar = (al * x_ref[...] + be * t_ref[...]) * over
    turned = split(al * g_ref[...] + be * h_ref[...])
    gram = (aa * k0_ref[...] + ab * k1_ref[...] + bb * e_ref[...]) * (over * over)
    for step in range(NS_STEPS):
        near = polar.astype(BF16)
        if step:
            gram = nt(near, near)
        polar = 1.5 * polar - 0.5 * nn(gram.astype(BF16), near)
    r_ref[...] = polar
    polar_copy = pltpu.make_async_copy(r_ref, polar_out.at[0, 0], out_sem.at[0])
    polar_copy.start()
    pair = split(polar)
    hands = []
    for at, part_of in enumerate((top, bottom)):
        weight = three(nn, (turned[0][part_of], turned[1][part_of]), pair)
        wsend[part_of] = weight.astype(BF16)
        hand = pltpu.make_async_remote_copy(
            src_ref=wsend.at[part_of], dst_ref=handed_out.at[0, 0, part_of],
            send_sem=seg_send.at[1 + at], recv_sem=seg_recv.at[1 + at],
            device_id={"seg": ahead}, device_id_type=MESH,
        )
        hands.append(hand)

        @pl.when(seg < segs - 1)
        def _():
            hand.start()

    @pl.when(seg == 0)
    def _():
        zero_ref[...] = jnp.zeros_like(zero_ref)
        clear = pltpu.make_async_copy(zero_ref, handed_out.at[0, 0], out_sem.at[1])
        clear.start()
        clear.wait()

    fetch.wait_send()
    for copy in sent:
        copy.wait_send()
    polar_copy.wait()
    lam_copy.wait()

    @pl.when(seg < segs - 1)
    def _():
        for hand in hands:
            hand.wait_send()

    @pl.when(seg > 0)
    def _():
        for hand in hands:
            hand.wait_recv()


def store(polar_in, handed_in, lam_in, polar_out, handed_out, lam_out, polar, handed, lam, sem):
    half = polar.shape[0] // 2
    ways = [
        (polar_in.at[0, 0, :half], polar.at[:half], polar_out.at[0, 0, :half]),
        (polar_in.at[0, 0, half:], polar.at[half:], polar_out.at[0, 0, half:]),
        (handed_in.at[0, 0], handed, handed_out.at[0, 0]),
        (lam_in, lam, lam_out),
    ]
    ins = [pltpu.make_async_copy(a, b, sem.at[0, n]) for n, (a, b, _) in enumerate(ways)]
    outs = [pltpu.make_async_copy(b, c, sem.at[1, n]) for n, (_, b, c) in enumerate(ways)]
    for copy in ins:
        copy.start()
    for first, second in zip(ins, outs):
        first.wait()
        second.start()
    for copy in outs:
        copy.wait()


def shards(segs, secs, left_env, right_env, left_piece, right_piece, guess, inverse_values,
           precond, sector_rows):
    channels, size = left_env.shape[2], left_env.shape[3]
    hbm = pl.BlockSpec(memory_space=pl.ANY)
    square = (size, size)
    envs = pltpu.VMEM((channels,) + square, BF16)
    block = pltpu.VMEM(square, BF16)
    wide = pltpu.VMEM((size, channels * size), BF16)
    five = pltpu.VMEM((5,) + square, BF16)
    full = pltpu.VMEM(square, F32)
    sems = pltpu.SemaphoreType.DMA
    outs = (
        jax.ShapeDtypeStruct((1, 1) + square, F32),
        jax.ShapeDtypeStruct((1, 1) + square, BF16),
        jax.ShapeDtypeStruct((1,), F32),
    )
    made = pl.pallas_call(
        functools.partial(kernel, segs, secs),
        out_shape=outs,
        in_specs=[hbm] * 8,
        out_specs=(hbm,) * 3,
        scratch_shapes=[
            envs, envs, block, block, pltpu.VMEM((1, size), F32), block,
            pltpu.SMEM((1, 1), jnp.int32), wide, wide,
            pltpu.VMEM((size, WD * size), BF16), block, block,
            five, five, five, five,
            pltpu.VMEM((3, 16, 128), F32), pltpu.VMEM((3, secs, 16, 128), F32), block,
        ] + [full] * 13 + [
            block, pltpu.SMEM((1,), F32),
            sems((7,)), sems((3,)), sems((3,)), sems((11,)), sems((11,)), sems((10,)), sems((10,)),
            sems((3, secs)), sems((3, secs)), sems((3,)),
        ],
        compiler_params=pltpu.CompilerParams(
            collective_id=0, has_side_effects=True, vmem_limit_bytes=60 * 1024 * 1024
        ),
        cost_estimate=pl.CostEstimate(
            flops=3 * 60 * 2 * size ** 3, bytes_accessed=6 * 1024 * 1024, transcendentals=0
        ),
    )(left_env, right_env, left_piece, right_piece, guess, inverse_values, precond, sector_rows)
    return pl.pallas_call(
        store, out_shape=outs, in_specs=[hbm] * 3, out_specs=(hbm,) * 3,
        scratch_shapes=[full, block, pltpu.SMEM((1,), F32), sems((2, 4))],
        compiler_params=pltpu.CompilerParams(vmem_limit_bytes=60 * 1024 * 1024),
    )(*made)


def solution(mesh):
    placed = (
        P("seg", "sec", None, None, None),
        P("seg", "sec", None, None, None),
        P("seg", "sec", None, None),
        P("seg", "sec", None, None),
        P("seg", "sec", None, None),
        P("seg", "sec", None),
        P("seg", "sec", None, None),
        P("seg", "sec"),
    )
    return jax.shard_map(
        functools.partial(shards, mesh.shape["seg"], mesh.shape["sec"]),
        mesh=mesh,
        in_specs=placed,
        out_specs=(P("seg", "sec", None, None), P("seg", "sec", None, None), P("seg")),
        check_vma=False,
    )
```
